256 devices in a mesh: replica: 32 (over z, x_lo, core), tensor: 8 (over x_hi, y).
Axes of the slice: x: 4 (x_hi: 2, x_lo: 2; x = x_hi * 2 + x_lo), y: 4, z: 8, core: 2. Of those that a mesh axis runs over, the one named last changes fastest.
Arguments:
- head_outputs: bfloat16 [16384, 4096], P('replica', 'tensor'), may hold values from -6 to 6
- output_weight: bfloat16 [32, 4096, 4096], P('replica', 'tensor'), may hold values from -0.09375 to 0.09375
- output_grad: bfloat16 [16384, 4096], P(('replica', 'tensor')), may hold values from -6 to 6
- outer_delta: float32 [32, 768, 4096], P('replica', 'tensor'), may hold values from -6 to 6
- local_slice: bfloat16 [32, 768, 4096], P('replica', 'tensor'), may hold values from -6 to 6
- global_slice: float32 [768, 4096], P('tensor', 'replica'), may hold values from -6 to 6
- momentum: float32 [768, 4096], P('tensor', 'replica'), may hold values from -4 to 4
Outputs:
- projected: bfloat16 [16384, 4096], P(('replica', 'tensor'))
- head_grads: bfloat16 [16384, 4096], P('replica', 'tensor')
- weight_grad: bfloat16 [32, 4096, 4096], P('replica', 'tensor')
- merged_slice: bfloat16 [32, 768, 4096], P('replica', 'tensor')
- new_global: float32 [768, 4096], P('tensor', 'replica')
- new_momentum: float32 [768, 4096], P('tensor', 'replica')
The draws below stay inside these ranges and needn't reach their ends.
All inputs are finite; a program needn't handle non-finite values.
Results may differ from the reference program's by a relative error of at most 0.017.
Values may be sent and summed in bfloat16 or wider, within the bound.
No kernel may reach another device: no remote copies, remote signals or barrier semaphores. Data moves between devices by JAX's collectives and lax.ppermute only.
A program may use at most 64 MiB of HBM per device.

```python
import jax
import jax.numpy as jnp
from jax import lax

DW = 4096
HQ = 4096
TOK_REP = 512
FR = 768
REPLICAS = 32
TOKENS = 16384
N_REPLICA = 32
N_TENSOR = 8


def with_spikes(array, key, source, target, blocks, factor):
    owner, partner = [(jnp.arange(array.shape[dim]) // (array.shape[dim] // blocks)).reshape([-1 if axis == dim else 1 for axis in range(array.ndim)]) for dim in (source, target)]
    chosen = jax.random.permutation(key, blocks)[partner]
    strong = (owner == chosen) | (owner == (partner + blocks // 2) % blocks)
    return jnp.where(strong, factor * array, array)


def block_scale(key, dims, cuts, least, top_value):
    def one(position, blocks):
        heights = jax.random.uniform(jax.random.fold_in(jax.random.fold_in(key, 6), position), (blocks,), jnp.float32, least / len(cuts), top_value / len(cuts))
        return jnp.repeat(jnp.exp(heights), dims[position] // blocks).reshape((-1,) + (1,) * (len(dims) - position - 1))

    loudness = one(*cuts[0])
    for cut in cuts[1:]:
        loudness = loudness * one(*cut)
    return loudness


def noise(rng, dims, deviation, reach, split=(), kind=jnp.bfloat16):
    loudness = block_scale(rng, dims, split, -0.22, 0.18) if split else 1.0
    array = jax.random.normal(rng, dims, jnp.float32) * deviation * loudness
    return jnp.minimum(jnp.maximum(array, -reach), reach).astype(kind)


def heavy_noise(key, shape, width, reach, cuts, heavy, dtype=jnp.bfloat16):
    drawn = width * jax.random.normal(key, shape, jnp.float32)
    if cuts:
        drawn = drawn * block_scale(key, shape, cuts, -0.22, 0.18)
    return jnp.clip(with_spikes(drawn, jax.random.fold_in(key, 3), *heavy), -reach, reach).astype(dtype)


def setup_inputs(seed: int = 0) -> dict:
    arg_keys = jax.random.split(jax.random.key(seed), 8)
    return {
        "head_outputs": noise(arg_keys[0], (TOKENS, HQ), 1.0, 6.0, ((0, 32), (1, 8))),
        "output_weight": noise(arg_keys[1], (REPLICAS, HQ, DW), HQ ** -0.5, 0.09375, ((0, 32), (1, 8))),
        "output_grad": noise(arg_keys[2], (TOKENS, DW), 1.0, 6.0, ((0, 256),)),
        "outer_delta": heavy_noise(arg_keys[3], (REPLICAS, FR, DW), 1.0, 6.0, ((0, 32), (1, 8)), (0, 2, 32, 2.75), jnp.float32),
        "local_slice": noise(arg_keys[4], (REPLICAS, FR, DW), 1.0, 6.0, ((0, 32), (1, 8))),
        "global_slice": noise(arg_keys[5], (FR, DW), 1.0, 6.0, ((0, 8), (1, 32)), jnp.float32),
        "momentum": noise(arg_keys[6], (FR, DW), 0.3, 4.0, ((0, 8), (1, 32)), jnp.float32),
    }


def one_replica(items):
    head_rows, weight, grad_rows = items
    parts = jnp.einsum('tnh,nhd->ntd', head_rows.reshape(TOK_REP, N_TENSOR, -1).astype(jnp.float32), weight.reshape(N_TENSOR, -1, DW).astype(jnp.float32))
    rounded = lax.optimization_barrier(parts.astype(jnp.bfloat16))
    projected = jnp.sum(rounded.astype(jnp.float32), axis=0).astype(jnp.bfloat16)
    head_grad = jnp.dot(grad_rows, weight.T, preferred_element_type=jnp.float32).astype(jnp.bfloat16)
    weight_grad = jnp.dot(head_rows.T, grad_rows, preferred_element_type=jnp.float32).astype(jnp.bfloat16)
    return projected, head_grad, weight_grad


def reference(head_outputs, output_weight, output_grad, outer_delta, local_slice, global_slice, momentum):
    head_rows = head_outputs.reshape(N_REPLICA, TOK_REP, HQ)
    grad_rows = output_grad.reshape(N_REPLICA, TOK_REP, DW)
    projected, head_grads, weight_grad = lax.map(one_replica, (head_rows, output_weight, grad_rows))
    rounded = lax.optimization_barrier(outer_delta.astype(jnp.bfloat16))
    mean_delta = jnp.sum(rounded.astype(jnp.float32), axis=0) / N_REPLICA
    new_momentum = 0.9 * momentum + mean_delta
    new_global = global_slice - 0.7 * (mean_delta + 0.9 * new_momentum)
    merged_slice = (0.5 * local_slice.astype(jnp.float32) + 0.5 * new_global[None]).astype(jnp.bfloat16)
    return (projected.reshape(TOKENS, DW), head_grads.reshape(TOKENS, HQ), weight_grad, merged_slice, new_global, new_momentum)
```

```python
import functools

import jax
import jax.numpy as jnp
from jax import lax
from jax.experimental import pallas as pl
from jax.experimental.pallas import tpu as pltpu
from jax.sharding import PartitionSpec as P

BF = jnp.bfloat16
F32 = jnp.float32
NY, NX = 4, 2
CX = 2560
CB = 512
LANE = 128
ORDER = (0, 3, 1, 2)
VMEM_LIMIT = 48 * 1024 * 1024


def call(kernel, outs, *args, **kw):
    params = pltpu.CompilerParams(vmem_limit_bytes=VMEM_LIMIT)
    cost = kw.pop("cost", None)
    if cost is None:
        size = sum(a.size * a.dtype.itemsize for a in args) + sum(
            o.size * o.dtype.itemsize for o in jax.tree.leaves(outs)
        )
        cost = pl.CostEstimate(flops=0, bytes_accessed=size, transcendentals=0)
    return pl.pallas_call(
        kernel, out_shape=outs, compiler_params=params, cost_estimate=cost, **kw
    )(*args)


def sds(*shape, dtype=BF):
    return jax.ShapeDtypeStruct(shape, dtype)


def send_y(x, step):
    pairs = [(k * NY + y, k * NY + (y + step) % NY) for k in range(NX) for y in range(NY)]
    return lax.ppermute(x, "tensor", pairs)


def send_x(x):
    pairs = [(k * NY + y, (1 - k) * NY + y) for k in range(NX) for y in range(NY)]
    return lax.ppermute(x, "tensor", pairs)


def send_replica(x, bit):
    return lax.ppermute(x, "replica", [(r, r ^ bit) for r in range(lax.axis_size("replica"))])


def row_block(yi, xi):
    me = lax.axis_index("tensor")
    k, y = me // NY, me % NY
    return ((k + xi) % NX) * NY + (y + ORDER[yi]) % NY


def arrange_rows(a_ref, rel_ref):
    for yi in range(NY):
        for xi in range(NX):
            at = pl.multiple_of(row_block(yi, xi) * 64, 64)
            rel_ref[pl.ds((yi * NX + xi) * 64, 64), :] = a_ref[pl.ds(at, 64), :]


def proj_kernel(a_ref, w_ref, p00, p01, pm, pp, p2a, p2b, py0, py1, rel):
    j = pl.program_id(0)

    @pl.when(j == 0)
    def _():
        arrange_rows(a_ref, rel)

    p = jnp.dot(rel[...], w_ref[...], preferred_element_type=F32).astype(BF)

    @pl.when(j < CX // CB)
    def _():
        p00[...] = p[0:64]
        p01[...] = p[64:128]
        pm[...] = p[128:256]
        pp[...] = p[256:384]
        p2a[...] = p[384:448]
        p2b[...] = p[448:512]

    @pl.when(j >= CX // CB)
    def _():
        for yi in range(NY):
            py0[pl.ds(yi * 64, 64), :] = p[yi * 128 : yi * 128 + 64]
            py1[pl.ds(yi * 64, 64), :] = p[yi * 128 + 64 : yi * 128 + 128]


def in_x(rows):
    return pl.BlockSpec((rows, CB), lambda j: (0, jnp.minimum(j, CX // CB - 1)))


def in_y(rows):
    return pl.BlockSpec((rows, CB), lambda j: (0, jnp.maximum(j - CX // CB, 0)))


def project(a, w):
    d = w.shape[1]
    cy = d - CX
    return call(
        proj_kernel,
        [sds(64, CX), sds(64, CX), sds(128, CX), sds(128, CX), sds(64, CX), sds(64, CX),
         sds(256, cy), sds(256, cy)],
        a, w,
        grid=(d // CB,),
        in_specs=[pl.BlockSpec((512, 512), lambda j: (0, 0)), pl.BlockSpec((512, CB), lambda j: (0, j))],
        out_specs=[in_x(64), in_x(64), in_x(128), in_x(128), in_x(64), in_x(64), in_y(256), in_y(256)],
        scratch_shapes=[pltpu.VMEM((512, 512), BF)],
        cost=pl.CostEstimate(flops=2 * 512 * 512 * d, bytes_accessed=9 << 20, transcendentals=0),
    )


def grads_kernel(a_ref, w_ref, x2, xm, xp, f1, f2, y4, yx, wg, hg, rel, relt, g, acc):
    j = pl.program_id(0)

    @pl.when(j == 0)
    def _():
        arrange_rows(a_ref, rel)
        relt[...] = rel[...].T
        acc[...] = jnp.zeros_like(acc)

    @pl.when(j < CX // CB)
    def _():
        g[0:128, :] = x2[...]
        g[128:256, :] = xm[...]
        g[256:384, :] = xp[...]
        g[384:448, :] = f1[...]
        g[448:512, :] = f2[...]

    @pl.when(j >= CX // CB)
    def _():
        for yi in range(NY):
            g[yi * 128 : yi * 128 + 64, :] = y4[yi * 64 : yi * 64 + 64, :]
            g[yi * 128 + 64 : yi * 128 + 128, :] = yx[yi * 64 : yi * 64 + 64, :]

    wg[...] = jnp.dot(relt[...], g[...], preferred_element_type=F32).astype(BF)
    acc[...] += lax.dot_general(
        g[...], w_ref[...], (((1,), (1,)), ((), ())), preferred_element_type=F32
    )

    @pl.when(j == pl.num_programs(0) - 1)
    def _():
        for yi in range(NY):
            for xi in range(NX):
                at = pl.multiple_of(row_block(yi, xi) * 64, 64)
                hg[pl.ds(at, 64), :] = acc[pl.ds((yi * NX + xi) * 64, 64), :].astype(BF)


def grads(a, w, x2, xm, xp, f1, f2, y4, yx):
    d = w.shape[1]
    full = pl.BlockSpec((512, 512), lambda j: (0, 0))
    col = pl.BlockSpec((512, CB), lambda j: (0, j))
    return call(
        grads_kernel,
        [sds(512, d), sds(512, 512)],
        a, w, x2, xm, xp, f1, f2, y4, yx,
        grid=(d // CB,),
        in_specs=[full, col, in_x(128), in_x(128), in_x(128), in_x(64), in_x(64), in_y(256), in_y(256)],
        out_specs=[col, full],
        scratch_shapes=[
            pltpu.VMEM((512, 512), BF),
            pltpu.VMEM((512, 512), BF),
            pltpu.VMEM((512, CB), BF),
            pltpu.VMEM((512, 512), F32),
        ],
        cost=pl.CostEstimate(flops=4 * 512 * 512 * d, bytes_accessed=14 << 20, transcendentals=0),
    )


def gather_grad(g):
    gx, gy = g[:, :CX], g[:, CX:]
    x1 = send_x(gx)
    ym = send_y(gy, 1)
    yp = send_y(gy, -1)
    x2 = jnp.concatenate([gx, x1], 0)
    xm = send_y(x2, 1)
    xp = send_y(x2, -1)
    y2 = send_y(ym, 1)
    f1 = send_y(xm[:64], 1)
    f2 = send_y(xp[64:], -1)
    y4 = jnp.concatenate([gy, ym, yp, y2], 0)
    yx = send_x(y4)
    return x2, xm, xp, f1, f2, y4, yx


def f32(x):
    return x[...].astype(F32)


def add_low(p_ref, r_ref, o_ref):
    o_ref[0:64, :] = (f32(p_ref.at[0:64, :]) + f32(r_ref)).astype(BF)
    o_ref[64:128, :] = p_ref[64:128, :]


def add_high(p_ref, r_ref, o_ref):
    o_ref[0:64, :] = p_ref[0:64, :]
    o_ref[64:128, :] = (f32(p_ref.at[64:128, :]) + f32(r_ref)).astype(BF)


def cross_kernel(p01, sp, sm, q1):
    q1[...] = (f32(p01) + f32(sp.at[64:128, :]) + f32(sm.at[64:128, :])).astype(BF)


def split_y_kernel(py0, yx, q0, qm, qp, q2):
    for yi, out in enumerate((q0, qm, qp, q2)):
        rows = slice(yi * 64, yi * 64 + 64)
        out[...] = (f32(py0.at[rows, :]) + f32(yx.at[rows, :])).astype(out.dtype)


def add_kernel(a, b, o):
    o[...] = (f32(a) + f32(b)).astype(o.dtype)


def finish_kernel(p00, sp, sm, x, q0, s1, s2, o):
    o[:, 0:CX] = (
        f32(p00) + f32(sp.at[0:64, :]) + f32(sm.at[0:64, :]) + f32(x)
    ).astype(BF)
    o[:, CX:] = (f32(q0) + f32(s1) + f32(s2)).astype(BF)


def scatter_projected(pieces, d):
    p00, p01, pm, pp, p2a, p2b, py0, py1 = pieces
    cy = d - CX
    yx = send_x(py1)
    r1 = send_y(p2a, 1)
    r2 = send_y(p2b, -1)
    pp = call(add_low, sds(128, CX), pp, r1)
    pm = call(add_high, sds(128, CX), pm, r2)
    sp = send_y(pp, 1)
    sm = send_y(pm, -1)
    q0, qm, qp, q2 = call(
        split_y_kernel,
        [sds(64, cy, dtype=F32), sds(64, cy, dtype=F32), sds(64, cy), sds(64, cy)],
        py0, yx,
    )
    w = send_y(q2, -1)
    s1 = send_y(qp, 1)
    qm = call(add_kernel, sds(64, cy), qm, w)
    s2 = send_y(qm, -1)
    x = send_x(call(cross_kernel, sds(64, CX), p01, sp, sm))
    return call(finish_kernel, sds(64, d), p00, sp, sm, x, q0, s1, s2)


def bits():
    r = lax.axis_index("replica")
    return r // 4, (r // 2) % 2, r % 2


def lanes(block):
    start = block * LANE
    return pl.ds(start if isinstance(start, int) else pl.multiple_of(start, LANE), LANE)


def core_send_kernel(d_ref, send):
    _, _, c = bits()
    for i in range(send.shape[1] // LANE):
        send[:, lanes(i)] = d_ref[:, lanes(2 * i + 1 - c)].astype(BF)


def core_add_kernel(d_ref, recv, keep, send):
    _, x, c = bits()
    for i in range(keep.shape[1] // LANE):
        for out, k in ((send, 2 * i + 1 - x), (keep, 2 * i + x)):
            mine = d_ref[:, lanes(2 * k + c)].astype(BF).astype(F32)
            out[:, lanes(i)] = (mine + f32(recv.at[:, lanes(k)])).astype(out.dtype)


def x_add_kernel(keep, recv, glob, mom, total, send):
    n = keep.shape[1]
    t = f32(keep) + f32(recv)
    total[...] = t
    send[:, 0:n] = t.astype(BF)
    send[:, n:] = (glob[...] - 0.567 * mom[...]).astype(BF)


def z_add_kernel(level, keep, mine, recv, total, send):
    n = keep.shape[1]
    z, _, _ = bits()
    bit = (z // level) % 2
    t = f32(keep) + f32(recv.at[:, 0:n])
    total[...] = t
    send[:, 0:n] = t.astype(BF)
    for i in range(level):
        send[:, lanes(n // LANE + bit * level + i)] = mine[:, lanes(n // LANE + i)]
        send[:, lanes(n // LANE + (1 - bit) * level + i)] = recv[:, lanes(n // LANE + i)]


def update_kernel(replicas, level, keep, mine, recv, glob, mom, quarter, new_glob, new_mom):
    n = keep.shape[1]
    z, _, _ = bits()
    bit = (z // level) % 2
    for src, half in ((mine, bit), (recv, 1 - bit)):
        for i in range(level):
            at = lanes(half * level + i)
            mean = (keep[:, at] + f32(recv.at[:, at])) / replicas
            h = f32(src.at[:, lanes(n // LANE + i)])
            quarter[:, at] = (h - 1.33 * mean).astype(BF)
    at = lanes(z)
    mean = (keep[:, at] + f32(recv.at[:, at])) / replicas
    momentum = 0.9 * mom[...] + mean
    new_mom[...] = momentum
    new_glob[...] = glob[...] - 0.7 * (mean + 0.9 * momentum)


def merge_kernel(local, q00, q01, q10, q11, o):
    _, x, c = bits()
    for dx, dc, q in ((0, 0, q00), (0, 1, q01), (1, 0, q10), (1, 1, q11)):
        for i in range(q.shape[1] // LANE):
            xx = x + dx - 2 * x * dx
            cc = c + dc - 2 * c * dc
            at = lanes(4 * i + 2 * xx + cc)
            o[:, at] = (0.5 * f32(local.at[:, at]) + 0.5 * f32(q.at[:, lanes(i)])).astype(BF)


def outer_work(delta, local, glob, mom):
    replicas = lax.axis_size("replica")
    rows, d = delta.shape
    n = d // 4
    recv = send_replica(call(core_send_kernel, sds(rows, d // 2), delta), 1)
    keep, send = call(core_add_kernel, [sds(rows, n, dtype=F32), sds(rows, n)], delta, recv)
    recv = send_replica(send, 2)
    keep, mine = call(
        x_add_kernel, [sds(rows, n, dtype=F32), sds(rows, n + LANE)], keep, recv, glob, mom
    )
    for level in (1, 2):
        recv = send_replica(mine, 4 * level)
        keep, mine = call(
            functools.partial(z_add_kernel, level),
            [sds(rows, n, dtype=F32), sds(rows, n + 2 * level * LANE)],
            keep, mine, recv,
        )
    recv = send_replica(mine, 16)
    small = sds(*glob.shape, dtype=F32)
    q00, new_glob, new_mom = call(
        functools.partial(update_kernel, replicas, 4),
        [sds(rows, n), small, small],
        keep, mine, recv, glob, mom,
    )
    q01 = send_replica(q00, 1)
    q10 = send_replica(q00, 2)
    q11 = send_replica(q10, 1)
    merged = call(merge_kernel, sds(rows, d), local, q00, q01, q10, q11)
    return merged, new_glob, new_mom


def on_device(
    head_outputs, output_weight, output_grad, outer_delta, local_slice, global_slice, momentum
):
    weight = output_weight[0]
    gathered = gather_grad(output_grad)
    pieces = project(head_outputs, weight)
    projected = scatter_projected(pieces, weight.shape[1])
    merged, new_global, new_momentum = outer_work(
        outer_delta[0], local_slice[0], global_slice, momentum
    )
    weight_grad, head_grads = grads(head_outputs, weight, *gathered)
    return (projected, head_grads, weight_grad[None], merged[None], new_global, new_momentum)


def solution(mesh):
    in_specs = (
        P("replica", "tensor"),
        P("replica", "tensor", None),
        P(("replica", "tensor"), None),
        P("replica", "tensor", None),
        P("replica", "tensor", None),
        P("tensor", "replica"),
        P("tensor", "replica"),
    )
    out_specs = (
        P(("replica", "tensor"), None),
        P("replica", "tensor"),
        P("replica", "tensor", None),
        P("replica", "tensor", None),
        P("tensor", "replica"),
        P("tensor", "replica"),
    )
    return jax.shard_map(
        on_device, mesh=mesh, in_specs=in_specs, out_specs=out_specs, check_vma=False
    )
```

```python
import functools

import jax
import jax.numpy as jnp
from jax import lax
from jax.experimental import pallas as pl
from jax.experimental.pallas import tpu as pltpu
from jax.sharding import PartitionSpec as P

BF = jnp.bfloat16
F32 = jnp.float32
NY, NX = 4, 2
CX = 2560
CB = 512
LANE = 128
ORDER = (0, 3, 1, 2)
Y_LEFT, Y_RIGHT = slice(2560, 3328), slice(3328, 4096)
VMEM_LIMIT = 24 * 1024 * 1024


def call(kernel, outs, *args, deps=(), cost=None, **kw):
    if cost is None:
        size = sum(a.size * a.dtype.itemsize for a in (*args, *jax.tree.leaves(outs)))
        cost = pl.CostEstimate(flops=0, bytes_accessed=size, transcendentals=0)
    if "in_specs" not in kw:
        vmem = pl.BlockSpec(memory_space=pltpu.VMEM)
        kw.update(in_specs=[vmem] * len(args), out_specs=jax.tree.map(lambda _: vmem, outs))
    kw["in_specs"] = kw["in_specs"] + [pl.BlockSpec(memory_space=pl.ANY)] * len(deps)

    def body(*refs):
        kernel(*refs[: len(args)], *refs[len(args) + len(deps) :])

    return pl.pallas_call(
        body, out_shape=outs, cost_estimate=cost,
        compiler_params=pltpu.CompilerParams(vmem_limit_bytes=VMEM_LIMIT), **kw
    )(*args, *deps)


def sds(*shape, dtype=BF):
    return jax.ShapeDtypeStruct(shape, dtype)


def send_y(x, step):
    pairs = [(k * NY + y, k * NY + (y + step) % NY) for k in range(NX) for y in range(NY)]
    return lax.ppermute(x, "tensor", pairs)


def send_x(x):
    pairs = [(k * NY + y, (1 - k) * NY + y) for k in range(NX) for y in range(NY)]
    return lax.ppermute(x, "tensor", pairs)


def send_replica(x, bit):
    return lax.ppermute(x, "replica", [(r, r ^ bit) for r in range(lax.axis_size("replica"))])


def row_block(yi, xi):
    me = lax.axis_index("tensor")
    k, y = me // NY, me % NY
    return ((k + xi) % NX) * NY + (y + ORDER[yi]) % NY


def arrange_rows(a_ref, rel_ref):
    for yi in range(NY):
        for xi in range(NX):
            at = pl.multiple_of(row_block(yi, xi) * 64, 64)
            rel_ref[pl.ds((yi * NX + xi) * 64, 64), :] = a_ref[pl.ds(at, 64), :]


def blocks(first, last):
    return [slice(k, k + CB) for k in range(first, last, CB)]


def dot(x, y):
    return jnp.dot(x, y, preferred_element_type=F32).astype(BF)


def early_kernel(a_hbm, w_hbm, rel, w, p2a, p2b, py1, a, sems):
    d = w.shape[1]
    order = blocks(CX, d) + blocks(0, CX)
    copies = [pltpu.make_async_copy(a_hbm, a, sems.at[len(order)])]
    for i, k in enumerate(order):
        at = pl.ds(k.start, CB)
        copies.append(pltpu.make_async_copy(w_hbm.at[:, at], w.at[:, at], sems.at[i]))
    for copy in copies:
        copy.start()
    copies[0].wait()
    arrange_rows(a, rel)
    turned = jnp.concatenate([rel[yi * 128 + 64 : yi * 128 + 128, :] for yi in range(NY)], 0)
    for copy, k in zip(copies[1:], order):
        copy.wait()
        if k.start >= CX:
            py1[:, k.start - CX : k.stop - CX] = dot(turned, w[:, k])
        else:
            p = dot(rel[384:512, :], w[:, k])
            p2a[:, k] = p[0:64]
            p2b[:, k] = p[64:128]


def early(a, w, deps):
    d = w.shape[1]
    hbm, vmem = pl.BlockSpec(memory_space=pl.ANY), pl.BlockSpec(memory_space=pltpu.VMEM)
    return call(
        early_kernel,
        [sds(512, 512), sds(512, d), sds(64, CX), sds(64, CX), sds(256, d - CX)],
        a, w, deps=deps,
        in_specs=[hbm, hbm],
        out_specs=[vmem] * 5,
        scratch_shapes=[pltpu.VMEM((512, 512), BF), pltpu.SemaphoreType.DMA((d // CB + 1,))],
        cost=pl.CostEstimate(flops=0, bytes_accessed=12 << 20, transcendentals=0),
    )


def late_kernel(rel, w, p00, p01, pm, pp, py0):
    d = w.shape[1]
    for k in blocks(0, CX):
        p = dot(rel[0:384, :], w[:, k])
        p00[:, k] = p[0:64]
        p01[:, k] = p[64:128]
        pm[:, k] = p[128:256]
        pp[:, k] = p[256:384]
    kept = jnp.concatenate([rel[yi * 128 : yi * 128 + 64, :] for yi in range(NY)], 0)
    for k in blocks(CX, d):
        py0[:, k.start - CX : k.stop - CX] = dot(kept, w[:, k])


def grads_kernel(rel, w, gg, x1, ym, mu, yp, md, fu, fd, y4, yx, wg_hbm, hg, wg, g, sems):
    d = w.shape[1]
    across = rel[...].T
    copies = []
    for i, k in enumerate(blocks(0, d)):
        if k.start < CX:
            near, far = (slice(n * CX + k.start, n * CX + k.stop) for n in (1, 2))
            parts = (gg[:, k], x1[:, k], ym[:, k], mu[:, near], yp[:, k], md[:, near], fu[:, far], fd[:, far])
        else:
            cols = slice(k.start - CX, k.stop - CX)
            parts = [r[yi * 64 : yi * 64 + 64, cols] for yi in range(NY) for r in (y4, yx)]
        for n, p in enumerate(parts):
            g[n * 64 : n * 64 + 64, k] = p
        wg[:, k] = dot(across, g[:, k])
        at = pl.ds(k.start, CB)
        copies.append(pltpu.make_async_copy(wg.at[:, at], wg_hbm.at[:, at], sems.at[i]))
        copies[-1].start()
    h = lax.dot_general(
        g[...], w[...], (((1,), (1,)), ((), ())), preferred_element_type=F32
    ).astype(BF)
    for yi in range(NY):
        for xi in range(NX):
            at = pl.multiple_of(row_block(yi, xi) * 64, 64)
            n = (yi * NX + xi) * 64
            hg[pl.ds(at, 64), :] = h[n : n + 64]
    for copy in copies:
        copy.wait()


def grads(rel, w, *parts, deps):
    d = w.shape[1]
    hbm, vmem = pl.BlockSpec(memory_space=pl.ANY), pl.BlockSpec(memory_space=pltpu.VMEM)
    return call(
        grads_kernel,
        [sds(512, d), sds(512, 512)],
        rel, w, *parts, deps=deps,
        in_specs=[vmem] * (2 + len(parts)),
        out_specs=[hbm, vmem],
        scratch_shapes=[
            pltpu.VMEM((512, d), BF),
            pltpu.VMEM((512, d), BF),
            pltpu.SemaphoreType.DMA((d // CB,)),
        ],
        cost=pl.CostEstimate(flops=0, bytes_accessed=16 << 20, transcendentals=0),
    )


def f32(x):
    return x[...].astype(F32)


def copy_kernel(x, o):
    o[...] = x[...]


def core_split_kernel(d_ref, keep, send):
    _, _, c = bits()
    for i in range(send.shape[1] // LANE):
        keep[:, lanes(i)] = d_ref[:, lanes(2 * i + c)].astype(BF)
        send[:, lanes(i)] = d_ref[:, lanes(2 * i + 1 - c)].astype(BF)


def round2_kernel(p2a, p2b, x1, ym, yp, up, down):
    for out, p, y, cols in ((up, p2a, ym, Y_LEFT), (down, p2b, yp, Y_RIGHT)):
        out[:, 0:CX] = p[...]
        out[:, CX : 2 * CX] = x1[...]
        out[:, 2 * CX :] = y[:, cols]


def round3_kernel(pp, pm, mu, md, ym, g, yp, py0, yx, up, down, y4, q0, qp, qm):
    def q(yi):
        rows = slice(yi * 64, yi * 64 + 64)
        return f32(py0.at[rows, :]) + f32(yx.at[rows, :])

    q0[...] = q(0)
    qm[...] = q(1)
    qp[...] = q(2)
    q2 = q(3).astype(BF)
    half = (g.shape[1] - CX) // 2
    up[:, 0:CX] = (f32(pp.at[0:64, :]) + f32(mu.at[:, 0:CX])).astype(BF)
    up[:, CX : 2 * CX] = pp[64:128, :]
    up[:, 2 * CX : 3 * CX] = ym[:, 0:CX]
    up[:, 3 * CX :] = q2[:, 0:half]
    down[:, 0:CX] = pm[0:64, :]
    down[:, CX : 2 * CX] = (f32(pm.at[64:128, :]) + f32(md.at[:, 0:CX])).astype(BF)
    down[:, 2 * CX : 3 * CX] = md[:, CX : 2 * CX]
    down[:, 3 * CX :] = q2[:, half:]
    for i, r in enumerate((g, ym, yp)):
        y4[i * 64 : i * 64 + 64, :] = r[:, CX:]
    y4[192:256, 0:half] = mu[:, 2 * CX :]
    y4[192:256, half:] = md[:, 2 * CX :]


def round4_kernel(p01, fu, fd, qp, qm, up, down, x):
    half = qp.shape[1] // 2
    x[...] = (f32(p01) + f32(fu.at[:, CX : 2 * CX]) + f32(fd.at[:, CX : 2 * CX])).astype(BF)
    up[:, 0:half] = (qp[:, 0:half] + f32(fu.at[:, 3 * CX :])).astype(BF)
    up[:, half:] = qp[:, half:].astype(BF)
    down[:, 0:half] = qm[:, 0:half].astype(BF)
    down[:, half:] = (qm[:, half:] + f32(fd.at[:, 3 * CX :])).astype(BF)


def finish_kernel(p00, sp, sm, x, q0, s1, s2, o):
    o[:, 0:CX] = (
        f32(p00) + f32(sp.at[:, 0:CX]) + f32(sm.at[:, 0:CX]) + f32(x)
    ).astype(BF)
    o[:, CX:] = (f32(q0) + f32(s1) + f32(s2)).astype(BF)


def bits():
    r = lax.axis_index("replica")
    return r // 4, (r // 2) % 2, r % 2


def lanes(block):
    start = block * LANE
    return pl.ds(start if isinstance(start, int) else pl.multiple_of(start, LANE), LANE)


def core_add_kernel(mine, recv, keep, send):
    _, x, _ = bits()
    for i in range(keep.shape[1] // LANE):
        for out, k in ((send, 2 * i + 1 - x), (keep, 2 * i + x)):
            out[:, lanes(i)] = (f32(mine.at[:, lanes(k)]) + f32(recv.at[:, lanes(k)])).astype(out.dtype)


def x_add_kernel(keep, recv, glob, mom, total, send):
    n = keep.shape[1]
    t = f32(keep) + f32(recv)
    total[...] = t
    send[:, 0:n] = t.astype(BF)
    send[:, n:] = (glob[...] - 0.567 * mom[...]).astype(BF)


def z_bit(level):
    z, _, _ = bits()
    return (z // level) % 2


def z_add_kernel(level, keep, mine, recv, total, send):
    n = keep.shape[1]
    bit = z_bit(level)
    t = f32(keep) + f32(recv.at[:, 0:n])
    total[...] = t
    send[:, 0:n] = t.astype(BF)
    for i in range((mine.shape[1] - n) // LANE):
        send[:, lanes(n // LANE + 2 * i + bit)] = mine[:, lanes(n // LANE + i)]
        send[:, lanes(n // LANE + 2 * i + 1 - bit)] = recv[:, lanes(n // LANE + i)]


def update_kernel(replicas, level, keep, mine, recv, glob, mom, quarter, new_glob, new_mom):
    n = keep.shape[1]
    z, _, _ = bits()
    bit = z_bit(level)
    for src, side in ((mine, bit), (recv, 1 - bit)):
        for i in range((mine.shape[1] - n) // LANE):
            at = lanes(2 * i + side)
            mean = (keep[:, at] + f32(recv.at[:, at])) / replicas
            h = f32(src.at[:, lanes(n // LANE + i)])
            quarter[:, at] = (h - 1.33 * mean).astype(BF)
    at = lanes(z)
    mean = (keep[:, at] + f32(recv.at[:, at])) / replicas
    momentum = 0.9 * mom[...] + mean
    new_mom[...] = momentum
    new_glob[...] = glob[...] - 0.7 * (mean + 0.9 * momentum)


def merge_kernel(local, q00, q01, q10, q11, o):
    _, x, c = bits()
    for dx, dc, q in ((0, 0, q00), (0, 1, q01), (1, 0, q10), (1, 1, q11)):
        for i in range(q.shape[1] // LANE):
            xx = x + dx - 2 * x * dx
            cc = c + dc - 2 * c * dc
            at = lanes(4 * i + 2 * xx + cc)
            o[:, at] = (0.5 * f32(local.at[:, at]) + 0.5 * f32(q.at[:, lanes(i)])).astype(BF)


def on_device(
    head_outputs, output_weight, output_grad, outer_delta, local_slice, global_slice, momentum
):
    heads, weight, delta, local = head_outputs, output_weight[0], outer_delta[0], local_slice[0]
    replicas = lax.axis_size("replica")
    rows, d = delta.shape
    cy, n = d - CX, d // 4

    def part(fn, *fixed):
        return functools.partial(fn, *fixed)

    def f(*shape):
        return sds(*shape, dtype=F32)

    x1 = send_x(output_grad[:, :CX])
    ym = send_y(output_grad, 1)
    yp = send_y(output_grad, -1)
    keep, send = call(core_split_kernel, [sds(rows, d // 2)] * 2, delta)
    c1 = send_replica(send, 1)
    keep, send = call(core_add_kernel, [f(rows, n), sds(rows, n)], keep, c1)
    xl = send_replica(send, 2)

    rel, w, p2a, p2b, py1 = early(heads, weight, (send,))
    yx = send_x(py1)

    up, down = call(
        round2_kernel, [sds(64, 2 * CX + cy // 2)] * 2, p2a, p2b, x1, ym, yp, deps=(py1, xl)
    )
    mu, md = send_y(up, 1), send_y(down, -1)
    keep, mine = call(
        x_add_kernel, [f(rows, n), sds(rows, n + LANE)], keep, xl, global_slice, momentum, deps=(up,)
    )
    z4 = send_replica(mine, 16)
    p00, p01, pm, pp, py0 = call(
        late_kernel,
        [sds(64, CX), sds(64, CX), sds(128, CX), sds(128, CX), sds(256, cy)],
        rel, w, deps=(mine,),
        cost=pl.CostEstimate(flops=0, bytes_accessed=8 << 20, transcendentals=0),
    )
    keep, mine = call(
        part(z_add_kernel, 4), [f(rows, n), sds(rows, n + 2 * LANE)], keep, mine, z4, deps=(py0,)
    )
    z2 = send_replica(mine, 8)

    up, down, y4, q0, qp, qm = call(
        round3_kernel,
        [sds(64, 3 * CX + cy // 2)] * 2 + [sds(256, cy)] + [f(64, cy)] * 3,
        pp, pm, mu, md, ym, output_grad, yp, py0, yx, deps=(mine,),
    )
    fu, fd = send_y(up, 1), send_y(down, -1)
    gyx = send_x(y4)
    keep, mine = call(
        part(z_add_kernel, 2), [f(rows, n), sds(rows, n + 4 * LANE)], keep, mine, z2, deps=(y4,)
    )
    z1 = send_replica(mine, 4)
    q00, new_global, new_momentum = call(
        part(update_kernel, replicas, 1), [sds(rows, n), f(*momentum.shape), f(*momentum.shape)],
        keep, mine, z1, global_slice, momentum,
    )
    q01 = send_replica(q00, 1)
    q10 = call(copy_kernel, sds(rows, n), send_replica(q00, 2))
    q11 = send_replica(q10, 1)

    up, down, x = call(
        round4_kernel, [sds(64, cy), sds(64, cy), sds(64, CX)], p01, fu, fd, qp, qm, deps=(q10,)
    )
    s1, s2 = send_y(up, 1), send_y(down, -1)
    x = send_x(x)
    weight_grad, head_grads = grads(
        rel, w, output_grad, x1, ym, mu, yp, md, fu, fd, y4, gyx, deps=(up,)
    )
    merged = call(merge_kernel, sds(rows, d), local, q00, q01, q10, q11, deps=(head_grads,))
    projected = call(finish_kernel, sds(64, d), p00, fu, fd, x, q0, s1, s2, deps=(merged,))
    return (projected, head_grads, weight_grad[None], merged[None], new_global, new_momentum)


def solution(mesh):
    in_specs = (
        P("replica", "tensor"),
        P("replica", "tensor", None),
        P(("replica", "tensor"), None),
        P("replica", "tensor", None),
        P("replica", "tensor", None),
        P("tensor", "replica"),
        P("tensor", "replica"),
    )
    out_specs = (
        P(("replica", "tensor"), None),
        P("replica", "tensor"),
        P("replica", "tensor", None),
        P("replica", "tensor", None),
        P("tensor", "replica"),
        P("tensor", "replica"),
    )
    return jax.shard_map(
        on_device, mesh=mesh, in_specs=in_specs, out_specs=out_specs, check_vma=False
    )
```

```python
import functools

import jax
import jax.numpy as jnp
from jax import lax
from jax.experimental import pallas as pl
from jax.experimental.pallas import tpu as pltpu
from jax.sharding import PartitionSpec as P

BF = jnp.bfloat16
F32 = jnp.float32
NY, NX = 4, 2
CX = 2560
CB = 512
LANE = 128
ORDER = (0, 3, 1, 2)
Y_LEFT, Y_RIGHT = slice(2560, 3328), slice(3328, 4096)
EARLY_COST = pl.CostEstimate(flops=0, bytes_accessed=64 << 20, transcendentals=0)
COST = pl.CostEstimate(flops=1, bytes_accessed=1024, transcendentals=0)
VMEM_LIMIT = 20 * 1024 * 1024


def call(kernel, outs, *args, deps=(), cost=COST, **kw):
    if "in_specs" not in kw:
        vmem = pl.BlockSpec(memory_space=pltpu.VMEM)
        kw.update(in_specs=[vmem] * len(args), out_specs=jax.tree.map(lambda _: vmem, outs))
    kw["in_specs"] = kw["in_specs"] + [pl.BlockSpec(memory_space=pl.ANY)] * len(deps)

    def body(*refs):
        kernel(*refs[: len(args)], *refs[len(args) + len(deps) :])

    return pl.pallas_call(
        body, out_shape=outs, cost_estimate=cost,
        compiler_params=pltpu.CompilerParams(vmem_limit_bytes=VMEM_LIMIT), **kw
    )(*args, *deps)


def sds(*shape, dtype=BF):
    return jax.ShapeDtypeStruct(shape, dtype)


def send_y(x, step):
    pairs = [(k * NY + y, k * NY + (y + step) % NY) for k in range(NX) for y in range(NY)]
    return lax.ppermute(x, "tensor", pairs)


def send_x(x):
    pairs = [(k * NY + y, (1 - k) * NY + y) for k in range(NX) for y in range(NY)]
    return lax.ppermute(x, "tensor", pairs)


def send_replica(x, bit):
    return lax.ppermute(x, "replica", [(r, r ^ bit) for r in range(lax.axis_size("replica"))])


def row_block(yi, xi):
    me = lax.axis_index("tensor")
    k, y = me // NY, me % NY
    return ((k + xi) % NX) * NY + (y + ORDER[yi]) % NY


def arrange_rows(a_ref, rel_ref):
    for yi in range(NY):
        for xi in range(NX):
            at = pl.multiple_of(row_block(yi, xi) * 64, 64)
            rel_ref[pl.ds((yi * NX + xi) * 64, 64), :] = a_ref[pl.ds(at, 64), :]


def blocks(first, last):
    return [slice(k, k + CB) for k in range(first, last, CB)]


def dot(x, y):
    return jnp.dot(x, y, preferred_element_type=F32).astype(BF)


def early_kernel(a, w, rel, p2a, p2b, py1):
    d = w.shape[1]
    arrange_rows(a, rel)
    turned = jnp.concatenate([rel[yi * 128 + 64 : yi * 128 + 128, :] for yi in range(NY)], 0)
    for k in blocks(CX, d):
        py1[:, k.start - CX : k.stop - CX] = dot(turned, w[:, k])
    for k in blocks(0, CX):
        p = dot(rel[384:512, :], w[:, k])
        p2a[:, k] = p[0:64]
        p2b[:, k] = p[64:128]


def late_kernel(rel, w, p00, p01, pm, pp, py0):
    d = w.shape[1]
    for k in blocks(0, CX):
        p = dot(rel[0:384, :], w[:, k])
        p00[:, k] = p[0:64]
        p01[:, k] = p[64:128]
        pm[:, k] = p[128:256]
        pp[:, k] = p[256:384]
    kept = jnp.concatenate([rel[yi * 128 : yi * 128 + 64, :] for yi in range(NY)], 0)
    for k in blocks(CX, d):
        py0[:, k.start - CX : k.stop - CX] = dot(kept, w[:, k])


def dot_nt(x, y):
    return lax.dot_general(x, y, (((1,), (1,)), ((), ())), preferred_element_type=F32)


def grads_x_kernel(rel, w, gg, x1, ym, mu, yp, md, part_wg, part_hg, g):
    for n, (r, first) in enumerate(((gg, 0), (x1, 0), (ym, 0), (mu, CX), (yp, 0), (md, CX))):
        g[n * 64 : n * 64 + 64, :] = r[:, first : first + CX]
    across = rel[0:384, :].T
    for k in blocks(0, CX):
        part_wg[:, k] = jnp.dot(across, g[:, k], preferred_element_type=F32)
    part_hg[...] = dot_nt(g[...], w[:, 0:CX])


def grads_y_kernel(rel, w, y4, yx, wg_hbm, part_hg, wg, g, sems):
    across = rel[...].T
    copies = []
    for i, k in enumerate(blocks(0, y4.shape[1])):
        for n in range(NY):
            g[n * 128 : n * 128 + 64, k] = y4[n * 64 : n * 64 + 64, k]
            g[n * 128 + 64 : n * 128 + 128, k] = yx[n * 64 : n * 64 + 64, k]
        wg[:, k] = dot(across, g[:, k])
        copies.append(
            pltpu.make_async_copy(
                wg.at[:, pl.ds(k.start, CB)], wg_hbm.at[:, pl.ds(CX + k.start, CB)], sems.at[i]
            )
        )
        copies[-1].start()
    part_hg[...] = dot_nt(g[...], w[:, CX:])
    for copy in copies:
        copy.wait()


def grads_y(rel, w, y4, yx, deps):
    d, cy = w.shape[1], y4.shape[1]
    hbm, vmem = pl.BlockSpec(memory_space=pltpu.HBM), pl.BlockSpec(memory_space=pltpu.VMEM)
    return call(
        grads_y_kernel, [sds(512, d), sds(512, 512, dtype=F32)], rel, w, y4, yx, deps=deps,
        in_specs=[vmem] * 4,
        out_specs=[hbm, vmem],
        scratch_shapes=[
            pltpu.VMEM((512, cy), BF),
            pltpu.VMEM((512, cy), BF),
            pltpu.SemaphoreType.DMA((len(blocks(0, cy)),)),
        ],
    )


def last_grads_kernel(old, rel, w, fu, fd, part_wg, hx, hy, wg_hbm, hg, done, wg, sems):
    across = rel[384:512, :].T
    done[...] = jnp.zeros_like(done)
    last = jnp.concatenate([r[:, 2 * CX : 3 * CX] for r in (fu, fd)], 0)
    copies = []
    for i, k in enumerate(blocks(0, CX)):
        more = jnp.dot(across, last[:, k], preferred_element_type=F32)
        wg[:, k] = (part_wg[:, k] + more).astype(BF)
        at = pl.ds(k.start, CB)
        copies.append(pltpu.make_async_copy(wg.at[:, at], wg_hbm.at[:, at], sems.at[i]))
        copies[-1].start()
    more = dot_nt(last, w[:, 0:CX])
    for yi in range(NY):
        for xi in range(NX):
            at = pl.ds(pl.multiple_of(row_block(yi, xi) * 64, 64), 64)
            n = (yi * NX + xi) * 64
            rows = hx[n : n + 64, :] if yi < 3 else more[xi * 64 : xi * 64 + 64]
            hg[at, :] = (hy[n : n + 64, :] + rows).astype(BF)
    for copy in copies:
        copy.wait()


def last_grads(old, rel, w, fu, fd, part_wg, hx, hy, deps):
    d = w.shape[1]
    hbm, vmem = pl.BlockSpec(memory_space=pltpu.HBM), pl.BlockSpec(memory_space=pltpu.VMEM)
    return call(
        last_grads_kernel,
        [sds(512, d), sds(512, 512), sds(8, LANE, dtype=F32)],
        old, rel, w, fu, fd, part_wg, hx, hy, deps=deps,
        in_specs=[hbm] + [vmem] * 7,
        out_specs=[hbm, vmem, vmem],
        input_output_aliases={0: 0},
        scratch_shapes=[pltpu.VMEM((512, CX), BF), pltpu.SemaphoreType.DMA((len(blocks(0, CX)),))],
    )


def f32(x):
    return x[...].astype(F32)


def copy_kernel(x, o):
    o[...] = x[...]


def core_split_kernel(d_ref, keep, send):
    _, _, c = bits()
    for i in range(send.shape[1] // LANE):
        keep[:, lanes(i)] = d_ref[:, lanes(2 * i + c)].astype(BF)
        send[:, lanes(i)] = d_ref[:, lanes(2 * i + 1 - c)].astype(BF)


def round2_kernel(p2a, p2b, x1, ym, yp, py1, up, down, turn):
    turn[...] = py1[...]
    for out, p, y, cols in ((up, p2a, ym, Y_LEFT), (down, p2b, yp, Y_RIGHT)):
        out[:, 0:CX] = p[...]
        out[:, CX : 2 * CX] = x1[...]
        out[:, 2 * CX :] = y[:, cols]


def round3_kernel(pp, pm, mu, md, ym, g, yp, py0, yx, up, down, y4, q0, qp, qm):
    def q(yi):
        rows = slice(yi * 64, yi * 64 + 64)
        return f32(py0.at[rows, :]) + f32(yx.at[rows, :])

    q0[...] = q(0)
    qm[...] = q(1)
    qp[...] = q(2)
    q2 = q(3).astype(BF)
    half = (g.shape[1] - CX) // 2
    up[:, 0:CX] = (f32(pp.at[0:64, :]) + f32(mu.at[:, 0:CX])).astype(BF)
    up[:, CX : 2 * CX] = pp[64:128, :]
    up[:, 2 * CX : 3 * CX] = ym[:, 0:CX]
    up[:, 3 * CX :] = q2[:, 0:half]
    down[:, 0:CX] = pm[0:64, :]
    down[:, CX : 2 * CX] = (f32(pm.at[64:128, :]) + f32(md.at[:, 0:CX])).astype(BF)
    down[:, 2 * CX : 3 * CX] = md[:, CX : 2 * CX]
    down[:, 3 * CX :] = q2[:, half:]
    for i, r in enumerate((g, ym, yp)):
        y4[i * 64 : i * 64 + 64, :] = r[:, CX:]
    y4[192:256, 0:half] = mu[:, 2 * CX :]
    y4[192:256, half:] = md[:, 2 * CX :]


def round4_kernel(p01, fu, fd, qp, qm, up, down, x):
    cy = qp.shape[1]
    half = cy // 2
    x[...] = (f32(p01) + f32(fu.at[:, CX : 2 * CX]) + f32(fd.at[:, CX : 2 * CX])).astype(BF)
    up[:, 0:half] = (qp[:, 0:half] + f32(fu.at[:, 3 * CX :])).astype(BF)
    up[:, half:cy] = qp[:, half:].astype(BF)
    down[:, 0:half] = qm[:, 0:half].astype(BF)
    down[:, half:cy] = (qm[:, half:] + f32(fd.at[:, 3 * CX :])).astype(BF)
    up[:, cy:] = jnp.zeros((64, LANE), BF)
    down[:, cy:] = jnp.zeros((64, LANE), BF)


def finish_kernel(p00, sp, sm, x, q0, s1, s2, o):
    o[:, 0:CX] = (
        f32(p00) + f32(sp.at[:, 0:CX]) + f32(sm.at[:, 0:CX]) + f32(x)
    ).astype(BF)
    cy = q0.shape[1]
    o[:, CX:] = (f32(q0) + f32(s1.at[:, 0:cy]) + f32(s2.at[:, 0:cy])).astype(BF)


def bits():
    r = lax.axis_index("replica")
    return r // 4, (r // 2) % 2, r % 2


def lanes(block):
    start = block * LANE
    return pl.ds(start if isinstance(start, int) else pl.multiple_of(start, LANE), LANE)


def core_add_kernel(mine, recv, keep, send):
    _, x, _ = bits()
    for i in range(keep.shape[1] // LANE):
        for out, k in ((send, 2 * i + 1 - x), (keep, 2 * i + x)):
            out[:, lanes(i)] = (f32(mine.at[:, lanes(k)]) + f32(recv.at[:, lanes(k)])).astype(out.dtype)


def x_add_kernel(keep, recv, glob, mom, total, send):
    n = keep.shape[1]
    t = f32(keep) + f32(recv)
    total[...] = t
    send[:, 0:n] = t.astype(BF)
    send[:, n:] = (glob[...] - 0.567 * mom[...]).astype(BF)


def z_bit(level):
    z, _, _ = bits()
    return (z // level) % 2


def z_add_kernel(level, keep, mine, recv, total, send):
    n = keep.shape[1]
    bit = z_bit(level)
    t = f32(keep) + f32(recv.at[:, 0:n])
    total[...] = t
    send[:, 0:n] = t.astype(BF)
    for i in range((mine.shape[1] - n) // LANE):
        send[:, lanes(n // LANE + 2 * i + bit)] = mine[:, lanes(n // LANE + i)]
        send[:, lanes(n // LANE + 2 * i + 1 - bit)] = recv[:, lanes(n // LANE + i)]


def update_kernel(replicas, level, keep, mine, recv, glob, mom, quarter, new_glob, new_mom):
    n = keep.shape[1]
    z, _, _ = bits()
    bit = z_bit(level)
    for src, side in ((mine, bit), (recv, 1 - bit)):
        for i in range((mine.shape[1] - n) // LANE):
            at = lanes(2 * i + side)
            mean = (keep[:, at] + f32(recv.at[:, at])) / replicas
            h = f32(src.at[:, lanes(n // LANE + i)])
            quarter[:, at] = (h - 1.33 * mean).astype(BF)
    at = lanes(z)
    mean = (keep[:, at] + f32(recv.at[:, at])) / replicas
    momentum = 0.9 * mom[...] + mean
    new_mom[...] = momentum
    new_glob[...] = glob[...] - 0.7 * (mean + 0.9 * momentum)


def merge_kernel(local, q00, q01, q10, q11, o):
    _, x, c = bits()
    for dx, dc, q in ((0, 0, q00), (0, 1, q01), (1, 0, q10), (1, 1, q11)):
        for i in range(q.shape[1] // LANE):
            xx = x + dx - 2 * x * dx
            cc = c + dc - 2 * c * dc
            at = lanes(4 * i + 2 * xx + cc)
            o[:, at] = (0.5 * f32(local.at[:, at]) + 0.5 * f32(q.at[:, lanes(i)])).astype(BF)


def on_device(
    head_outputs, output_weight, output_grad, outer_delta, local_slice, global_slice, momentum
):
    heads, weight, delta, local = head_outputs, output_weight[0], outer_delta[0], local_slice[0]
    replicas = lax.axis_size("replica")
    rows, d = delta.shape
    cy, n = d - CX, d // 4

    def part(fn, *fixed):
        return functools.partial(fn, *fixed)

    def f(*shape):
        return sds(*shape, dtype=F32)

    x1 = send_x(output_grad[:, :CX])
    ym = send_y(output_grad, 1)
    yp = send_y(output_grad, -1)
    keep, send = call(core_split_kernel, [sds(rows, d // 2)] * 2, delta)
    c1 = send_replica(send, 1)
    rel, p2a, p2b, py1 = call(
        early_kernel, [sds(512, 512), sds(64, CX), sds(64, CX), sds(256, cy)], heads, weight,
        cost=EARLY_COST,
    )
    w = weight
    keep, send = call(core_add_kernel, [f(rows, n), sds(rows, n)], keep, c1, deps=(py1,))
    xl = send_replica(send, 2)

    up, down, py1 = call(
        round2_kernel, [sds(64, 2 * CX + cy // 2)] * 2 + [sds(256, cy)],
        p2a, p2b, x1, ym, yp, py1, deps=(xl,),
    )
    mu, md = send_y(up, 1), send_y(down, -1)
    yx = send_x(py1)
    keep, mine = call(
        x_add_kernel, [f(rows, n), sds(rows, n + LANE)], keep, xl, global_slice, momentum, deps=(up,)
    )
    z4 = send_replica(mine, 16)
    p00, p01, pm, pp, py0 = call(
        late_kernel,
        [sds(64, CX), sds(64, CX), sds(128, CX), sds(128, CX), sds(256, cy)],
        rel, w, deps=(mine,),
    )
    keep, mine = call(
        part(z_add_kernel, 4), [f(rows, n), sds(rows, n + 2 * LANE)], keep, mine, z4, deps=(py0,)
    )
    z2 = send_replica(mine, 8)

    up, down, y4, q0, qp, qm = call(
        round3_kernel,
        [sds(64, 3 * CX + cy // 2)] * 2 + [sds(256, cy)] + [f(64, cy)] * 3,
        pp, pm, mu, md, ym, output_grad, yp, py0, yx, deps=(mine,),
    )
    fu, fd = send_y(up, 1), send_y(down, -1)
    gyx = send_x(y4)
    part_wg, part_hx = call(
        grads_x_kernel, [f(512, CX), f(384, 512)], rel, w, output_grad, x1, ym, mu, yp, md,
        deps=(y4,), scratch_shapes=[pltpu.VMEM((384, CX), BF)],
    )
    keep, mine = call(
        part(z_add_kernel, 2), [f(rows, n), sds(rows, n + 4 * LANE)], keep, mine, z2, deps=(part_hx,)
    )
    z1 = send_replica(mine, 4)
    q00, new_global, new_momentum = call(
        part(update_kernel, replicas, 1), [sds(rows, n), f(*momentum.shape), f(*momentum.shape)],
        keep, mine, z1, global_slice, momentum,
    )
    q01 = send_replica(q00, 1)
    weight_grad, part_hy = grads_y(rel, w, y4, gyx, deps=(q00,))
    q10 = send_replica(q00, 2)

    up, down, x = call(
        round4_kernel, [sds(64, cy + LANE), sds(64, cy + LANE), sds(64, CX)], p01, fu, fd, qp, qm, deps=(part_hy,)
    )
    s1, s2 = send_y(up, 1), send_y(down, -1)
    x = send_x(x)
    q10 = call(copy_kernel, sds(rows, n), q10, deps=(up,))
    q11 = send_replica(q10, 1)
    weight_grad, head_grads, done = last_grads(
        weight_grad, rel, w, fu, fd, part_wg, part_hx, part_hy, deps=(up,)
    )
    merged = call(merge_kernel, sds(rows, d), local, q00, q01, q10, q11, deps=(done,))
    projected = call(finish_kernel, sds(64, d), p00, fu, fd, x, q0, s1, s2, deps=(done,))
    return (projected, head_grads, weight_grad[None], merged[None], new_global, new_momentum)


def solution(mesh):
    in_specs = (
        P("replica", "tensor"),
        P("replica", "tensor", None),
        P(("replica", "tensor"), None),
        P("replica", "tensor", None),
        P("replica", "tensor", None),
        P("tensor", "replica"),
        P("tensor", "replica"),
    )
    out_specs = (
        P(("replica", "tensor"), None),
        P("replica", "tensor"),
        P("replica", "tensor", None),
        P("replica", "tensor", None),
        P("tensor", "replica"),
        P("tensor", "replica"),
    )
    return jax.shard_map(
        on_device, mesh=mesh, in_specs=in_specs, out_specs=out_specs, check_vma=False
    )
```
